32 devices in a mesh: freq: 4 (over z), src: 8 (over y, x, core).
Axes of the slice: x: 2, y: 2, z: 4, core: 2. Of those that a mesh axis runs over, the one named last changes fastest.
Arguments:
- jones: bfloat16 [1, 128, 8, 128, 1024], P(None, None, None, 'freq', 'src'), may hold values from -3 to 3
- directions: float32 [1, 3, 1024], P(None, None, 'src'), may hold values from -1 to 1
- brightness: float32 [1024], P('src'), may hold values from 0.1 to 4
- spectral: float32 [1024], P('src'), may hold values from 0 to 2.5
- antennas: float32 [3, 128], replicated, may hold values from -50 to 50
- visible: int32 [1, 512], replicated, may hold values from 0 to 1023, as said below
- pairs: int32 [2, 256], replicated, may hold values from 0 to 127, as said below
- group_of: int32 [256], replicated, may hold values from 0 to 63, as said below
Outputs:
- spectra: float32 [64, 1, 4, 128], P(('freq', 'src'))
The draws below stay inside these ranges and needn't reach their ends.
Inputs may be any that keep to these rules, and one draw needn't show every extreme that they name: `visible`: each row is sorted ascending without repeats. Its entries lie in a cyclic run of 640 consecutive catalog positions whose middle 512 - 512 // 4 positions are all present; for sidereal time 0 that run passes from 1023 to 0. pairs[0, n] < pairs[1, n]; no antenna pair repeats. `group_of`: never falls along the baselines; every group has a baseline. The groups of device d (in the order freq, src) are d * 2 to d * 2 + 1; their baselines number 2 to 14, exactly 14 on some device.
All inputs are finite; a program needn't handle non-finite values.
Results may differ from the reference program's by a relative error of at most 0.0032.
Values may be sent and summed in bfloat16 or wider, within the bound.
A program may use at most 64 MiB of HBM per device.

```python
import math
import jax
import jax.numpy as jnp
from jax import lax

NA = 128
NCH = 128
LSTS = 1
BD = 8
GD = 2
VIS = 512
CAT = 1024
NBL = 256
G = 64


def draw_visible(key, part):
    core_len = VIS - VIS // 4
    flank_len = VIS // 4
    per_list = []
    for sidereal in range(LSTS):
        key_start, key_pick = jax.random.split(jax.random.fold_in(key, 11 + sidereal))
        if sidereal == 0:
            run_start = jax.random.randint(key_start, (), CAT - core_len + 1, CAT)
        else:
            run_start = jax.random.randint(key_start, (), 0, CAT)
        core_run = run_start + jnp.arange(core_len)
        flank_cells = jnp.concatenate([run_start - flank_len + jnp.arange(flank_len), run_start + core_len + jnp.arange(flank_len)])
        picked = jax.random.permutation(key_pick, 2 * flank_len)[:flank_len]
        chosen = jnp.concatenate([core_run, flank_cells[picked]])
        per_list.append(jnp.sort(jnp.mod(chosen, CAT)))
    return jnp.stack(per_list).astype(jnp.int32)


def draw_pairs(key, part):
    total_pairs = NA * (NA - 1) // 2
    selected_indices = jax.random.permutation(jax.random.fold_in(key, 5), total_pairs)[:NBL]
    row_indices = jnp.arange(NA)
    row_offsets = row_indices * (2 * NA - row_indices - 1) // 2
    first_antenna = jnp.sum((row_offsets[None, 1:] <= selected_indices[:, None]).astype(jnp.int32), axis=1)
    second_antenna = selected_indices - row_offsets[first_antenna] + first_antenna + 1
    return jnp.stack([first_antenna, second_antenna]).astype(jnp.int32)


def draw_group_of(key, part):
    owners = G // GD
    pair_count = owners // 2
    key_extra, key_shuffle, key_moved = jax.random.split(jax.random.fold_in(key, 7), 3)
    extra = jax.random.randint(key_extra, (pair_count,), 0, BD - GD + 1)
    extra = jnp.where(jnp.arange(pair_count) == 0, BD - GD, extra)
    paired_loads = jnp.stack([BD + extra, BD - extra], axis=1).reshape(owners)
    owner_loads = paired_loads[jax.random.permutation(key_shuffle, owners)]
    base_size = owner_loads // GD
    leftover = owner_loads % GD
    group_sizes = base_size[:, None] + (jnp.arange(GD)[None, :] < leftover[:, None]).astype(jnp.int32)
    moved = jax.random.randint(key_moved, (owners, GD // 2), 0, 1 << 20) % base_size[:, None]
    group_sizes = group_sizes + jnp.stack([moved, -moved], axis=2).reshape(owners, GD)
    group_ends = jnp.cumsum(group_sizes.reshape(-1))
    baseline_ids = jnp.arange(NBL)
    return jnp.sum((group_ends[None, :] <= baseline_ids[:, None]).astype(jnp.int32), axis=1).astype(jnp.int32)


def block_scale(key, dims, pieces, smallest, top_value):
    level, own = 1.0, jax.random.fold_in(key, 6)
    for axis_at, parts in pieces:
        draws = jnp.exp(jax.random.uniform(jax.random.fold_in(own, axis_at), (parts,), jnp.float32, smallest / len(pieces), top_value / len(pieces)))
        level = level * jnp.repeat(draws, dims[axis_at] // parts).reshape([-1 if axis == axis_at else 1 for axis in range(len(dims))])
    return level


def normal_values(rng, dims, deviation, most, pieces=(), kind=jnp.bfloat16):
    entries = jax.random.normal(rng, dims, jnp.float32) * deviation
    if len(pieces) > 0:
        entries = block_scale(rng, dims, pieces, -0.22, 0.18) * entries
    return jnp.clip(entries, min=-most, max=most).astype(kind)


def setup_inputs(seed: int = 0) -> dict:
    key_list = jax.random.split(jax.random.key(seed), 9)
    jones = normal_values(key_list[0], (LSTS, NA, 8, NCH, CAT), 0.5, 3.0, ((3, 4), (4, 8)))
    directions = jnp.clip(jax.random.uniform(key_list[1], (LSTS, 3, CAT), jnp.float32, -1.0, 1.0) * block_scale(key_list[1], (LSTS, 3, CAT), ((2, 8),), -0.4, 0.0), -1.0, 1.0)
    brightness = jnp.clip(jnp.exp(math.log(4.0) - 3.6888794 * jax.random.uniform(key_list[2], (CAT,), jnp.float32) ** block_scale(key_list[2], (CAT,), ((0, 8),), -0.2, 0.2)), 0.1, 4.0)
    spectral = jnp.clip(2.5 * jax.random.uniform(key_list[3], (CAT,), jnp.float32) ** block_scale(key_list[3], (CAT,), ((0, 8),), -0.2, 0.2), 0.0, 2.5)
    antennas = jnp.clip(jax.random.uniform(key_list[4], (3, NA), jnp.float32, -50.0, 50.0), -50.0, 50.0)
    visible = draw_visible(jax.random.fold_in(key_list[8], 71), 0)
    pairs = draw_pairs(jax.random.fold_in(key_list[8], 71), 0)
    group_of = draw_group_of(jax.random.fold_in(key_list[8], 71), 0)
    return {"jones": jones, "directions": directions, "brightness": brightness, "spectral": spectral, "antennas": antennas, "visible": visible, "pairs": pairs, "group_of": group_of}


SPEED_LIGHT = 299792458.0
START_FREQ = 100000000.0
BAND_WIDTH = 100000000.0
PIVOT_FREQ = 150000000.0
HIGHEST = lax.Precision.HIGHEST

def channel_freq(channel, chan_count):
    return START_FREQ + channel.astype(jnp.float32) * (BAND_WIDTH / chan_count)

def geometry(antennas, directions):
    return antennas[0][:, None] * directions[0][None, :] + antennas[1][:, None] * directions[1][None, :] + antennas[2][:, None] * directions[2][None, :]

def channel_matrix(beam, geo_term, brightness, spectral, weight, frequency):
    phases = 2.0 * math.pi / SPEED_LIGHT * frequency * geo_term
    cos_grid = jnp.cos(phases)[:, None, None, :]
    sin_grid = jnp.sin(phases)[:, None, None, :]
    amplitude = jnp.sqrt(brightness * jnp.exp(-spectral * jnp.log(frequency / PIVOT_FREQ))) * weight
    antenna_total = beam.shape[0]
    beam_float = beam.astype(jnp.float32)
    beam_real = beam_float[:, 0:4].reshape(antenna_total, 2, 2, -1)
    beam_imag = beam_float[:, 4:8].reshape(antenna_total, 2, 2, -1)
    z_real = (amplitude * (beam_real * cos_grid + beam_imag * sin_grid)).reshape(2 * antenna_total, -1).astype(jnp.bfloat16)
    z_imag = (amplitude * (beam_imag * cos_grid - beam_real * sin_grid)).reshape(2 * antenna_total, -1).astype(jnp.bfloat16)
    left_side = jnp.concatenate([z_real, z_imag], axis=1)
    right_side = jnp.concatenate([left_side, jnp.concatenate([-z_imag, z_real], axis=1)], axis=0)
    return lax.dot_general(left_side, right_side, (((1,), (1,)), ((), ())), preferred_element_type=jnp.float32)

def selection_index(first_antenna, second_antenna, antenna_total):
    component = jnp.arange(8, dtype=jnp.int32)
    partition_indices = component // 4
    left_polarization = component % 4 // 2
    right_polarization = component % 2
    row_indices = first_antenna[None, :] * 2 + left_polarization[:, None]
    column_indices = partition_indices[:, None] * (2 * antenna_total) + second_antenna[None, :] * 2 + right_polarization[:, None]
    return (row_indices * (4 * antenna_total) + column_indices).astype(jnp.int32)

def delay_tables(chan_count):
    chan_ids = jnp.arange(chan_count, dtype=jnp.int32)
    angles = 2.0 * math.pi / chan_count * chan_ids.astype(jnp.float32)
    taper = 0.35875 - 0.48829 * jnp.cos(angles) + 0.14128 * jnp.cos(2.0 * angles) - 0.01168 * jnp.cos(3.0 * angles)
    wrapped = chan_ids[:, None] * chan_ids[None, :] % chan_count
    phases = 2.0 * math.pi / chan_count * wrapped.astype(jnp.float32)
    return (jnp.cos(phases) * taper[None, :], jnp.sin(phases) * taper[None, :])

def delay_power(vis_data):
    cos_table, sin_table = delay_tables(vis_data.shape[0])
    vis_real = vis_data[:, :, 0:4]
    vis_imag = vis_data[:, :, 4:8]
    pattern = 'uk,ktpb->utpb'
    delay_real = jnp.einsum(pattern, cos_table, vis_real, precision=HIGHEST) + jnp.einsum(pattern, sin_table, vis_imag, precision=HIGHEST)
    delay_imag = jnp.einsum(pattern, cos_table, vis_imag, precision=HIGHEST) - jnp.einsum(pattern, sin_table, vis_real, precision=HIGHEST)
    return delay_real * delay_real + delay_imag * delay_imag

def reference(jones, directions, brightness, spectral, antennas, visible, pairs, group_of):
    antenna_total = antennas.shape[1]
    pick_flat = selection_index(pairs[0], pairs[1], antenna_total)
    weight = jnp.ones((VIS,), jnp.float32)
    per_lst = []
    for sidereal in range(LSTS):
        chosen = visible[sidereal]
        geo_term = geometry(antennas, jnp.take(directions[sidereal], chosen, axis=1))
        bright = jnp.take(brightness, chosen)
        slopes = jnp.take(spectral, chosen)
        beams_here = jones[sidereal]

        def one_channel(channel):
            beam = jnp.take(lax.dynamic_index_in_dim(beams_here, channel, 2, keepdims=False), chosen, axis=2)
            matrix = channel_matrix(beam, geo_term, bright, slopes, weight, channel_freq(channel, NCH))
            return matrix.reshape(-1)[pick_flat]
        per_lst.append(lax.map(one_channel, jnp.arange(NCH, dtype=jnp.int32)))
    vis_all = jnp.stack(per_lst, axis=1)
    power_all = delay_power(vis_all)
    membership = (group_of[:, None] == jnp.arange(G, dtype=jnp.int32)[None, :]).astype(jnp.float32)
    totals = jnp.einsum('utpb,bg->gtpu', power_all, membership, precision=HIGHEST)
    counts = lax.optimization_barrier(jnp.sum(membership, axis=0))
    return totals / (counts[:, None, None, None] * (VIS * NCH))
```

```python
import functools
import math

import jax
import jax.numpy as jnp
import numpy as np
from jax import lax
from jax.experimental import pallas as pl
from jax.experimental.pallas import tpu as pltpu
from jax.sharding import PartitionSpec as P

GD = 2
SLOTS = 16
SPEED_LIGHT = 299792458.0
START_FREQ = 100000000.0
BAND_WIDTH = 100000000.0
PIVOT_FREQ = 150000000.0
HIGHEST = lax.Precision.HIGHEST
F32 = jnp.float32
BF16 = jnp.bfloat16
MESH = pl.DeviceIdType.MESH
ABLK = 16

SIN_C = [(-1.0) ** i / math.factorial(2 * i + 1) for i in range(6)]
COS_C = [(-1.0) ** i / math.factorial(2 * i) for i in range(7)]


def dot_t(a, b):
    return lax.dot_general(a, b, (((1,), (1,)), ((), ())), preferred_element_type=F32)


def cos_sin_turns(x):
    r = x - jnp.round(x)
    h = r * math.pi
    h2 = h * h
    s = SIN_C[-1]
    for c in SIN_C[-2::-1]:
        s = s * h2 + c
    s = s * h
    c_ = COS_C[-1]
    for c in COS_C[-2::-1]:
        c_ = c_ * h2 + c
    s2 = s + s
    return 1.0 - s2 * s, s2 * c_


def vis_kernel(
    nf, ns, chan_count,
    jones_ref, dir_ref, bright_ref, spec_ref, ant_ref, visible_ref, pairs_ref, group_ref,
    out_ref,
    zbuf, geo_ref, stepc_ref, steps_ref, amp_ref, oa_ref, ob_ref, vbuf,
):
    step = pl.program_id(0)
    steps = pl.num_programs(0)
    na = ant_ref.shape[1]
    kd = jones_ref.shape[3]
    sd = jones_ref.shape[4]
    nbl = pairs_ref.shape[1]
    vis_total = visible_ref.shape[1]
    df = BAND_WIDTH / chan_count
    chan_base = lax.axis_index("freq") * kd

    @pl.when(step == 0)
    def _():
        ants = jnp.transpose(
            jnp.concatenate([ant_ref[...], jnp.zeros((na - 3, na), F32)], axis=0)
        )
        dirs = dir_ref[0]
        geo = (
            ants[:, 0:1] * dirs[0:1, :]
            + ants[:, 1:2] * dirs[1:2, :]
            + ants[:, 2:3] * dirs[2:3, :]
        )
        geo_ref[...] = geo
        c8, s8 = cos_sin_turns(geo * (8.0 * df / SPEED_LIGHT))
        stepc_ref[...] = c8
        steps_ref[...] = s8
        at = lax.broadcasted_iota(jnp.int32, (sd, vis_total), 0) + lax.axis_index("src") * sd
        hit = (at == visible_ref[...]).astype(F32).astype(BF16)
        weight = dot_t(jnp.ones((8, vis_total), BF16), hit)[0:1]
        chan = lax.broadcasted_iota(jnp.int32, (kd, sd), 0) + chan_base
        freq = START_FREQ + chan.astype(F32) * df
        amp_ref[...] = (
            jnp.sqrt(bright_ref[...] * jnp.exp(-spec_ref[...] * jnp.log(freq / PIVOT_FREQ)))
            * weight
        )
        ids = lax.broadcasted_iota(jnp.int32, (na, nbl), 0)
        oa_ref[...] = (ids == pairs_ref[0:1, :]).astype(F32).astype(BF16)
        ob_ref[...] = (ids == pairs_ref[1:2, :]).astype(F32)

    chan8 = lax.broadcasted_iota(jnp.int32, (8, sd), 0) + chan_base
    turn_rate = (START_FREQ + chan8.astype(F32) * df) * (1.0 / SPEED_LIGHT)

    def build(i, carry):
        a = step * ABLK + i
        c, s = cos_sin_turns(geo_ref[pl.ds(a, 1), :] * turn_rate)
        cd = stepc_ref[pl.ds(a, 1), :]
        sdl = steps_ref[pl.ds(a, 1), :]
        cs, ss = [c], [s]
        for _ in range(kd // 8 - 1):
            c, s = c * cd - s * sdl, s * cd + c * sdl
            cs.append(c)
            ss.append(s)
        amp = amp_ref[...]
        ca = jnp.concatenate(cs, axis=0) * amp
        sa = jnp.concatenate(ss, axis=0) * amp
        rows = pl.ds(pl.multiple_of(a * kd, kd), kd)
        for pq in range(4):
            br = jones_ref[0, i, pq].astype(F32)
            bi = jones_ref[0, i, 4 + pq].astype(F32)
            zbuf[pq, rows, :] = br * ca + bi * sa
            zbuf[4 + pq, rows, :] = bi * ca - br * sa
        return carry

    lax.fori_loop(0, ABLK, build, 0, unroll=4)

    @pl.when(step == steps - 1)
    def _():
        def channel(k, carry):
            def z(r, p, q):
                return zbuf[4 * r + 2 * p + q, pl.ds(k, na, stride=kd), :].astype(BF16)

            zr = jnp.concatenate(
                [jnp.concatenate([z(0, p, 0), z(0, p, 1)], axis=1) for p in range(2)], axis=0
            )
            zi = jnp.concatenate(
                [jnp.concatenate([z(1, p, 0), z(1, p, 1)], axis=1) for p in range(2)], axis=0
            )
            left = jnp.concatenate([zr, zi], axis=1)
            turned = jnp.concatenate([zi, -zr], axis=1)
            oa = oa_ref[...]
            ob = ob_ref[...]
            rows = []
            for right in (left, turned):
                gram = dot_t(left, right).astype(BF16)
                for p in range(2):
                    picked = jnp.dot(
                        gram[:, p * na : (p + 1) * na], oa, preferred_element_type=F32
                    )
                    for p2 in range(2):
                        rows.append(
                            jnp.sum(
                                picked[p2 * na : (p2 + 1) * na] * ob, axis=0, keepdims=True
                            )
                        )
            vis = jnp.concatenate(rows, axis=0)
            for t in range(nbl // 128):
                vbuf[t, pl.ds(k, 8, stride=kd), :] = vis[:, t * 128 : (t + 1) * 128]
            return carry

        lax.fori_loop(0, kd, channel, 0)
        owner = group_ref[...] // GD
        devices = nf * ns
        mine = lax.broadcasted_iota(jnp.int32, (devices, nbl), 0) == owner
        mine_f = mine.astype(F32)
        before = lax.broadcasted_iota(jnp.int32, (nbl, nbl), 0) < lax.broadcasted_iota(
            jnp.int32, (nbl, nbl), 1
        )
        counts = jnp.dot(
            mine_f.astype(BF16), before.astype(F32).astype(BF16), preferred_element_type=F32
        )
        rank = jnp.sum(counts * mine_f, axis=0, keepdims=True).astype(jnp.int32)
        slot = ((owner % ns) * nf + owner // ns) * SLOTS + rank
        vals = jnp.concatenate([vbuf[t] for t in range(nbl // 128)], axis=1).astype(BF16)
        per = nf * SLOTS
        for j in range(ns):
            place = lax.broadcasted_iota(jnp.int32, (per, nbl), 0) + j * per
            hit = (place == slot).astype(F32).astype(BF16)
            out_ref[j] = dot_t(hit, vals).astype(BF16)


def local_vis(nf, ns, chan_count, jones, directions, bright, spec, antennas, visible, pairs, groups):
    na, kd, sd = jones.shape[1], jones.shape[3], jones.shape[4]
    nbl = pairs.shape[1]
    whole = lambda x: pl.BlockSpec(x.shape, lambda i: (0,) * x.ndim)
    small = (directions, bright, spec, antennas, visible, pairs, groups)
    out = jax.ShapeDtypeStruct((ns, nf * SLOTS, 8 * kd), BF16)
    return pl.pallas_call(
        functools.partial(vis_kernel, nf, ns, chan_count),
        grid=(na // ABLK,),
        out_shape=out,
        in_specs=[pl.BlockSpec((1, ABLK, 8, kd, sd), lambda i: (0, i, 0, 0, 0))]
        + [whole(x) for x in small],
        out_specs=pl.BlockSpec(out.shape, lambda i: (0, 0, 0)),
        scratch_shapes=[
            pltpu.VMEM((8, na * kd, sd), F32),
            pltpu.VMEM((na, sd), F32),
            pltpu.VMEM((na, sd), F32),
            pltpu.VMEM((na, sd), F32),
            pltpu.VMEM((kd, sd), F32),
            pltpu.VMEM((na, nbl), BF16),
            pltpu.VMEM((na, nbl), F32),
            pltpu.VMEM((nbl // 128, 8 * kd, 128), F32),
        ],
        compiler_params=pltpu.CompilerParams(vmem_limit_bytes=48 * 1024 * 1024),
    )(jones, *small)


def exchange_kernel(
    nf, ns, scale, w_ref, table_ref, group_ref, out_ref,
    rbuf, sbuf, zbuf, send1, recv1, send2, recv2,
):
    f = lax.axis_index("freq")
    j = lax.axis_index("src")
    kd = w_ref.shape[2] // 8

    barrier = pltpu.get_barrier_semaphore()
    for o in range(1, ns):
        pl.semaphore_signal(
            barrier, inc=1, device_id=(f, lax.rem(j + o, ns)), device_id_type=MESH
        )
    for o in range(1, nf):
        pl.semaphore_signal(
            barrier, inc=1, device_id=(lax.rem(f + o, nf), j), device_id_type=MESH
        )
    pl.semaphore_wait(barrier, ns + nf - 2)

    first = []
    for o in range(1, ns):
        to = lax.rem(j + o, ns)
        copy = pltpu.make_async_remote_copy(
            src_ref=w_ref.at[to],
            dst_ref=rbuf.at[o - 1],
            send_sem=send1.at[o - 1],
            recv_sem=recv1.at[o - 1],
            device_id=(f, to),
            device_id_type=MESH,
        )
        copy.start()
        first.append(copy)
    total = w_ref[j].astype(F32)
    for o in range(1, ns):
        first[o - 1].wait_recv()
        total = total + rbuf[o - 1].astype(F32)
    sbuf[...] = total.reshape(nf, SLOTS, 8 * kd)

    second = []
    for o in range(1, nf):
        to = lax.rem(f + o, nf)
        copy = pltpu.make_async_remote_copy(
            src_ref=sbuf.at[to],
            dst_ref=zbuf.at[f],
            send_sem=send2.at[o - 1],
            recv_sem=recv2.at[o - 1],
            device_id=(to, j),
            device_id_type=MESH,
        )
        copy.start()
        second.append(copy)
    zbuf[f] = sbuf[f]
    dev = f * ns + j
    groups = group_ref[...]
    shape = (8, 4 * SLOTS)
    row = lax.broadcasted_iota(jnp.int32, shape, 0)
    col = lax.broadcasted_iota(jnp.int32, shape, 1)
    mean = jnp.zeros(shape, F32)
    start = jnp.zeros((1, 1), F32)
    slot = (col % SLOTS).astype(F32)
    for g in range(GD):
        count = jnp.sum((groups == dev * GD + g).astype(F32), axis=1, keepdims=True)
        inside = (row // 4 == g) & (row % 4 == col // SLOTS)
        inside = inside & (slot >= start) & (slot < start + count)
        mean = mean + jnp.where(inside, 1.0 / (count * scale), 0.0)
        start = start + count
    for copy in second:
        copy.wait_recv()
    blocks = [zbuf[i] for i in range(nf)]
    vis = jnp.concatenate(
        [
            jnp.concatenate([b[:, c * kd : (c + 1) * kd] for b in blocks], axis=1)
            for c in range(8)
        ],
        axis=0,
    )
    both = jnp.dot(vis, table_ref[...], precision=HIGHEST, preferred_element_type=F32)
    nu = table_ref.shape[1] // 2
    half = 4 * SLOTS
    real = both[:half, :nu] + both[half:, nu:]
    imag = both[half:, :nu] - both[:half, nu:]
    power = real * real + imag * imag
    out_ref[...] = jnp.dot(mean, power, precision=HIGHEST, preferred_element_type=F32)
    for copy in first + second:
        copy.wait_send()


def exchange(nf, ns, scale, w, table, groups):
    kd = w.shape[2] // 8
    vmem = pl.BlockSpec(memory_space=pltpu.VMEM)
    return pl.pallas_call(
        functools.partial(exchange_kernel, nf, ns, scale),
        out_shape=jax.ShapeDtypeStruct((8, table.shape[1] // 2), F32),
        in_specs=[vmem] * 3,
        out_specs=vmem,
        scratch_shapes=[
            pltpu.VMEM((ns - 1, nf * SLOTS, 8 * kd), BF16),
            pltpu.VMEM((nf, SLOTS, 8 * kd), F32),
            pltpu.VMEM((nf, SLOTS, 8 * kd), F32),
            pltpu.SemaphoreType.DMA((ns - 1,)),
            pltpu.SemaphoreType.DMA((ns - 1,)),
            pltpu.SemaphoreType.DMA((nf - 1,)),
            pltpu.SemaphoreType.DMA((nf - 1,)),
        ],
        compiler_params=pltpu.CompilerParams(
            collective_id=0, has_side_effects=True, vmem_limit_bytes=16 * 1024 * 1024
        ),
    )(w, table, groups)


def delay_table(chan_count):
    k = np.arange(chan_count)
    angles = 2.0 * np.pi * k / chan_count
    taper = (
        0.35875
        - 0.48829 * np.cos(angles)
        + 0.14128 * np.cos(2.0 * angles)
        - 0.01168 * np.cos(3.0 * angles)
    )
    phases = 2.0 * np.pi * ((k[:, None] * k[None, :]) % chan_count) / chan_count
    both = np.concatenate([np.cos(phases), np.sin(phases)], axis=1) * taper[:, None]
    return both.astype(np.float32)


def per_device(nf, ns, jones, directions, brightness, spectral, antennas, visible, pairs, group_of):
    chan_count = jones.shape[3] * nf
    groups = group_of.reshape(1, -1)
    w = local_vis(
        nf, ns, chan_count, jones, directions, brightness.reshape(1, -1),
        spectral.reshape(1, -1), antennas, visible, pairs, groups,
    )
    table = jnp.asarray(delay_table(chan_count))
    out = exchange(nf, ns, float(visible.shape[1] * chan_count), w, table, groups)
    return out.reshape(GD, 1, 4, chan_count)


def solution(mesh):
    nf, ns = mesh.shape["freq"], mesh.shape["src"]
    return jax.shard_map(
        functools.partial(per_device, nf, ns),
        mesh=mesh,
        in_specs=(
            P(None, None, None, "freq", "src"),
            P(None, None, "src"),
            P("src"),
            P("src"),
            P(),
            P(),
            P(),
            P(),
        ),
        out_specs=P(("freq", "src"), None, None, None),
        check_vma=False,
    )
```

```python
import functools
import math

import jax
import jax.numpy as jnp
import numpy as np
from jax import lax
from jax.experimental import pallas as pl
from jax.experimental.pallas import tpu as pltpu
from jax.sharding import PartitionSpec as P

GD = 2
SLOTS = 16
SPEED_LIGHT = 299792458.0
START_FREQ = 100000000.0
BAND_WIDTH = 100000000.0
PIVOT_FREQ = 150000000.0
HIGHEST = lax.Precision.HIGHEST
F32 = jnp.float32
BF16 = jnp.bfloat16
MESH = pl.DeviceIdType.MESH
ABLK = 16
PAD = 8

SIN_C = [(-1.0) ** i / math.factorial(2 * i + 1) for i in range(6)]
COS_C = [(-1.0) ** i / math.factorial(2 * i) for i in range(7)]


def dot_t(a, b):
    return lax.dot_general(a, b, (((1,), (1,)), ((), ())), preferred_element_type=F32)


def cos_sin_turns(x):
    r = x - jnp.round(x)
    h = r * math.pi
    h2 = h * h
    s = SIN_C[-1]
    for c in SIN_C[-2::-1]:
        s = s * h2 + c
    s = s * h
    c_ = COS_C[-1]
    for c in COS_C[-2::-1]:
        c_ = c_ * h2 + c
    s2 = s + s
    return 1.0 - s2 * s, s2 * c_


def vis_kernel(
    nf, ns, chan_count,
    jones_ref, dir_ref, bright_ref, spec_ref, ant_ref, visible_ref, pairs_ref, group_ref,
    out_ref,
    zbuf, geo_ref, stepc_ref, steps_ref, amp_ref, oa_ref, ob_ref, vbuf,
):
    step = pl.program_id(0)
    steps = pl.num_programs(0)
    na = ant_ref.shape[1]
    kd = jones_ref.shape[3]
    sd = jones_ref.shape[4]
    nbl = pairs_ref.shape[1]
    vis_total = visible_ref.shape[1]
    df = BAND_WIDTH / chan_count
    chan_base = lax.axis_index("freq") * kd

    @pl.when(step == 0)
    def _():
        ants = jnp.transpose(
            jnp.concatenate([ant_ref[...], jnp.zeros((na - 3, na), F32)], axis=0)
        )
        dirs = dir_ref[0]
        geo = (
            ants[:, 0:1] * dirs[0:1, :]
            + ants[:, 1:2] * dirs[1:2, :]
            + ants[:, 2:3] * dirs[2:3, :]
        )
        geo_ref[...] = geo
        c8, s8 = cos_sin_turns(geo * (8.0 * df / SPEED_LIGHT))
        stepc_ref[...] = c8
        steps_ref[...] = s8
        at = lax.broadcasted_iota(jnp.int32, (sd, vis_total), 0) + lax.axis_index("src") * sd
        hit = (at == visible_ref[...]).astype(F32).astype(BF16)
        weight = dot_t(jnp.ones((8, vis_total), BF16), hit)[0:1]
        chan = lax.broadcasted_iota(jnp.int32, (kd, sd), 0) + chan_base
        freq = START_FREQ + chan.astype(F32) * df
        amp_ref[...] = (
            jnp.sqrt(bright_ref[...] * jnp.exp(-spec_ref[...] * jnp.log(freq / PIVOT_FREQ)))
            * weight
        )
        ids = lax.broadcasted_iota(jnp.int32, (na, nbl), 0)
        oa_ref[...] = (ids == pairs_ref[0:1, :]).astype(F32).astype(BF16)
        ob_ref[...] = (ids == pairs_ref[1:2, :]).astype(F32)

    chan8 = lax.broadcasted_iota(jnp.int32, (8, sd), 0) + chan_base
    turn_rate = (START_FREQ + chan8.astype(F32) * df) * (1.0 / SPEED_LIGHT)

    def build(i, carry):
        a = step * ABLK + i
        c, s = cos_sin_turns(geo_ref[pl.ds(a, 1), :] * turn_rate)
        cd = stepc_ref[pl.ds(a, 1), :]
        sdl = steps_ref[pl.ds(a, 1), :]
        cs, ss = [c], [s]
        for _ in range(kd // 8 - 1):
            c, s = c * cd - s * sdl, s * cd + c * sdl
            cs.append(c)
            ss.append(s)
        amp = amp_ref[...]
        ca = jnp.concatenate(cs, axis=0) * amp
        sa = jnp.concatenate(ss, axis=0) * amp
        rows = pl.ds(pl.multiple_of(a * (kd + PAD), 8), kd)
        for pq in range(4):
            br = jones_ref[0, i, pq].astype(F32)
            bi = jones_ref[0, i, 4 + pq].astype(F32)
            zbuf[pq, rows, :] = br * ca + bi * sa
            zbuf[4 + pq, rows, :] = bi * ca - br * sa
        return carry

    lax.fori_loop(0, ABLK, build, 0, unroll=4)

    @pl.when(step == steps - 1)
    def _():
        def channel(k, carry):
            def z(r, p, q):
                return zbuf[4 * r + 2 * p + q, pl.ds(k, na, stride=kd + PAD), :].astype(BF16)

            zr = jnp.concatenate(
                [jnp.concatenate([z(0, p, 0), z(0, p, 1)], axis=1) for p in range(2)], axis=0
            )
            zi = jnp.concatenate(
                [jnp.concatenate([z(1, p, 0), z(1, p, 1)], axis=1) for p in range(2)], axis=0
            )
            left = jnp.concatenate([zr, zi], axis=1)
            turned = jnp.concatenate([zi, -zr], axis=1)
            oa = oa_ref[...]
            ob = ob_ref[...]
            rows = []
            for right in (left, turned):
                gram = dot_t(left, right).astype(BF16)
                for p in range(2):
                    picked = jnp.dot(
                        gram[:, p * na : (p + 1) * na], oa, preferred_element_type=F32
                    )
                    for p2 in range(2):
                        rows.append(
                            jnp.sum(
                                picked[p2 * na : (p2 + 1) * na] * ob, axis=0, keepdims=True
                            )
                        )
            vis = jnp.concatenate(rows, axis=0)
            for t in range(nbl // 128):
                vbuf[t, pl.ds(k, 8, stride=kd), :] = vis[:, t * 128 : (t + 1) * 128]
            return carry

        lax.fori_loop(0, kd, channel, 0, unroll=8)
        owner = group_ref[...] // GD
        devices = nf * ns
        mine = lax.broadcasted_iota(jnp.int32, (devices, nbl), 0) == owner
        mine_f = mine.astype(F32)
        before = lax.broadcasted_iota(jnp.int32, (nbl, nbl), 0) < lax.broadcasted_iota(
            jnp.int32, (nbl, nbl), 1
        )
        counts = jnp.dot(
            mine_f.astype(BF16), before.astype(F32).astype(BF16), preferred_element_type=F32
        )
        rank = jnp.sum(counts * mine_f, axis=0, keepdims=True).astype(jnp.int32)
        slot = ((owner % ns) * nf + owner // ns) * SLOTS + rank
        vals = jnp.concatenate([vbuf[t] for t in range(nbl // 128)], axis=1).astype(BF16)
        per = nf * SLOTS
        for j in range(ns):
            place = lax.broadcasted_iota(jnp.int32, (per, nbl), 0) + j * per
            hit = (place == slot).astype(F32).astype(BF16)
            out_ref[j] = dot_t(hit, vals).astype(BF16)


def local_vis(nf, ns, chan_count, jones, directions, bright, spec, antennas, visible, pairs, groups):
    na, kd, sd = jones.shape[1], jones.shape[3], jones.shape[4]
    nbl = pairs.shape[1]
    whole = lambda x: pl.BlockSpec(x.shape, lambda i: (0,) * x.ndim)
    small = (directions, bright, spec, antennas, visible, pairs, groups)
    out = jax.ShapeDtypeStruct((ns, nf * SLOTS, 8 * kd), BF16)
    return pl.pallas_call(
        functools.partial(vis_kernel, nf, ns, chan_count),
        grid=(na // ABLK,),
        out_shape=out,
        in_specs=[pl.BlockSpec((1, ABLK, 8, kd, sd), lambda i: (0, i, 0, 0, 0))]
        + [whole(x) for x in small],
        out_specs=pl.BlockSpec(out.shape, lambda i: (0, 0, 0)),
        scratch_shapes=[
            pltpu.VMEM((8, na * (kd + PAD), sd), F32),
            pltpu.VMEM((na, sd), F32),
            pltpu.VMEM((na, sd), F32),
            pltpu.VMEM((na, sd), F32),
            pltpu.VMEM((kd, sd), F32),
            pltpu.VMEM((na, nbl), BF16),
            pltpu.VMEM((na, nbl), F32),
            pltpu.VMEM((nbl // 128, 8 * kd, 128), F32),
        ],
        compiler_params=pltpu.CompilerParams(vmem_limit_bytes=60 * 1024 * 1024),
    )(jones, *small)


def exchange_kernel(
    nf, ns, scale, w_ref, table_ref, group_ref, out_ref,
    rbuf, sbuf, zbuf, send1, recv1, send2, recv2,
):
    f = lax.axis_index("freq")
    j = lax.axis_index("src")
    kd = w_ref.shape[2] // 8

    barrier = pltpu.get_barrier_semaphore()
    for o in range(1, ns):
        pl.semaphore_signal(
            barrier, inc=1, device_id=(f, lax.rem(j + o, ns)), device_id_type=MESH
        )
    for o in range(1, nf):
        pl.semaphore_signal(
            barrier, inc=1, device_id=(lax.rem(f + o, nf), j), device_id_type=MESH
        )
    pl.semaphore_wait(barrier, ns + nf - 2)

    first = []
    for o in range(1, ns):
        to = lax.rem(j + o, ns)
        copy = pltpu.make_async_remote_copy(
            src_ref=w_ref.at[to],
            dst_ref=rbuf.at[o - 1],
            send_sem=send1.at[o - 1],
            recv_sem=recv1.at[o - 1],
            device_id=(f, to),
            device_id_type=MESH,
        )
        copy.start()
        first.append(copy)
    dev = f * ns + j
    groups = group_ref[...]
    shape = (8, 4 * SLOTS)
    row = lax.broadcasted_iota(jnp.int32, shape, 0)
    col = lax.broadcasted_iota(jnp.int32, shape, 1)
    mean = jnp.zeros(shape, F32)
    start = jnp.zeros((1, 1), F32)
    slot = (col % SLOTS).astype(F32)
    for g in range(GD):
        count = jnp.sum((groups == dev * GD + g).astype(F32), axis=1, keepdims=True)
        inside = (row // 4 == g) & (row % 4 == col // SLOTS)
        inside = inside & (slot >= start) & (slot < start + count)
        mean = mean + jnp.where(inside, 1.0 / (count * scale), 0.0)
        start = start + count
    total = w_ref[j].astype(F32)
    for o in range(1, ns):
        first[o - 1].wait_recv()
        total = total + rbuf[o - 1].astype(F32)
    sbuf[...] = total.reshape(nf, SLOTS, 8 * kd)

    second = []
    for o in range(1, nf):
        to = lax.rem(f + o, nf)
        copy = pltpu.make_async_remote_copy(
            src_ref=sbuf.at[to],
            dst_ref=zbuf.at[f],
            send_sem=send2.at[o - 1],
            recv_sem=recv2.at[o - 1],
            device_id=(to, j),
            device_id_type=MESH,
        )
        copy.start()
        second.append(copy)
    zbuf[f] = sbuf[f]
    for copy in second:
        copy.wait_recv()
    blocks = [zbuf[i] for i in range(nf)]
    vis = jnp.concatenate(
        [
            jnp.concatenate([b[:, c * kd : (c + 1) * kd] for b in blocks], axis=1)
            for c in range(8)
        ],
        axis=0,
    )
    both = jnp.dot(vis, table_ref[...], precision=HIGHEST, preferred_element_type=F32)
    nu = table_ref.shape[1] // 2
    half = 4 * SLOTS
    real = both[:half, :nu] + both[half:, nu:]
    imag = both[half:, :nu] - both[:half, nu:]
    power = real * real + imag * imag
    out_ref[...] = jnp.dot(mean, power, precision=HIGHEST, preferred_element_type=F32)
    for copy in first + second:
        copy.wait_send()


def exchange(nf, ns, scale, w, table, groups):
    kd = w.shape[2] // 8
    vmem = pl.BlockSpec(memory_space=pltpu.VMEM)
    return pl.pallas_call(
        functools.partial(exchange_kernel, nf, ns, scale),
        out_shape=jax.ShapeDtypeStruct((8, table.shape[1] // 2), F32),
        in_specs=[vmem] * 3,
        out_specs=vmem,
        scratch_shapes=[
            pltpu.VMEM((ns - 1, nf * SLOTS, 8 * kd), BF16),
            pltpu.VMEM((nf, SLOTS, 8 * kd), F32),
            pltpu.VMEM((nf, SLOTS, 8 * kd), F32),
            pltpu.SemaphoreType.DMA((ns - 1,)),
            pltpu.SemaphoreType.DMA((ns - 1,)),
            pltpu.SemaphoreType.DMA((nf - 1,)),
            pltpu.SemaphoreType.DMA((nf - 1,)),
        ],
        compiler_params=pltpu.CompilerParams(
            collective_id=0, has_side_effects=True, vmem_limit_bytes=16 * 1024 * 1024
        ),
    )(w, table, groups)


def delay_table(chan_count):
    k = np.arange(chan_count)
    angles = 2.0 * np.pi * k / chan_count
    taper = (
        0.35875
        - 0.48829 * np.cos(angles)
        + 0.14128 * np.cos(2.0 * angles)
        - 0.01168 * np.cos(3.0 * angles)
    )
    phases = 2.0 * np.pi * ((k[:, None] * k[None, :]) % chan_count) / chan_count
    both = np.concatenate([np.cos(phases), np.sin(phases)], axis=1) * taper[:, None]
    return both.astype(np.float32)


def per_device(nf, ns, jones, directions, brightness, spectral, antennas, visible, pairs, group_of):
    chan_count = jones.shape[3] * nf
    groups = group_of.reshape(1, -1)
    w = local_vis(
        nf, ns, chan_count, jones, directions, brightness.reshape(1, -1),
        spectral.reshape(1, -1), antennas, visible, pairs, groups,
    )
    table = jnp.asarray(delay_table(chan_count))
    out = exchange(nf, ns, float(visible.shape[1] * chan_count), w, table, groups)
    return out.reshape(GD, 1, 4, chan_count)


def solution(mesh):
    nf, ns = mesh.shape["freq"], mesh.shape["src"]
    return jax.shard_map(
        functools.partial(per_device, nf, ns),
        mesh=mesh,
        in_specs=(
            P(None, None, None, "freq", "src"),
            P(None, None, "src"),
            P("src"),
            P("src"),
            P(),
            P(),
            P(),
            P(),
        ),
        out_specs=P(("freq", "src"), None, None, None),
        check_vma=False,
    )
```

```python
import functools
import math

import jax
import jax.numpy as jnp
import numpy as np
from jax import lax
from jax.experimental import pallas as pl
from jax.experimental.pallas import tpu as pltpu
from jax.sharding import PartitionSpec as P

GD = 2
SLOTS = 16
SPEED_LIGHT = 299792458.0
START_FREQ = 100000000.0
BAND_WIDTH = 100000000.0
PIVOT_FREQ = 150000000.0
HIGHEST = lax.Precision.HIGHEST
F32 = jnp.float32
BF16 = jnp.bfloat16
MESH = pl.DeviceIdType.MESH
ABLK = 16
KC = 16
PAD = 8

SIN_C = [(-1.0) ** i / math.factorial(2 * i + 1) for i in range(6)]
COS_C = [(-1.0) ** i / math.factorial(2 * i) for i in range(7)]


def dot_t(a, b):
    return lax.dot_general(a, b, (((1,), (1,)), ((), ())), preferred_element_type=F32)


def cos_sin_turns(x):
    r = x - jnp.round(x)
    h = r * math.pi
    h2 = h * h
    s = SIN_C[-1]
    for c in SIN_C[-2::-1]:
        s = s * h2 + c
    s = s * h
    c_ = COS_C[-1]
    for c in COS_C[-2::-1]:
        c_ = c_ * h2 + c
    s2 = s + s
    return 1.0 - s2 * s, s2 * c_


def kernel(
    nf, ns, chan_count, scale,
    jones_ref, dir_ref, bright_ref, spec_ref, ant_ref, visible_ref, pairs_ref, group_ref,
    table_ref, out_ref,
    zbuf, geo_ref, stepc_ref, steps_ref, amp_ref, oa_ref, ob_ref, hit_ref, vbuf,
    wbuf, rbuf, sbuf, dbuf, send1, recv1, send2, recv2,
):
    step = pl.program_id(0)
    steps = pl.num_programs(0)
    na = ant_ref.shape[1]
    kd = jones_ref.shape[3]
    sd = jones_ref.shape[4]
    nbl = pairs_ref.shape[1]
    vis_total = visible_ref.shape[1]
    per = nf * SLOTS
    df = BAND_WIDTH / chan_count
    f = lax.axis_index("freq")
    j = lax.axis_index("src")
    chan_base = f * kd
    barrier = pltpu.get_barrier_semaphore()

    @pl.when(step == 0)
    def _():
        for o in range(1, ns):
            pl.semaphore_signal(
                barrier, inc=1, device_id=(f, lax.rem(j + o, ns)), device_id_type=MESH
            )
        for o in range(1, nf):
            pl.semaphore_signal(
                barrier, inc=1, device_id=(lax.rem(f + o, nf), j), device_id_type=MESH
            )
        ants = jnp.transpose(
            jnp.concatenate([ant_ref[...], jnp.zeros((na - 3, na), F32)], axis=0)
        )
        dirs = dir_ref[0]
        geo = (
            ants[:, 0:1] * dirs[0:1, :]
            + ants[:, 1:2] * dirs[1:2, :]
            + ants[:, 2:3] * dirs[2:3, :]
        )
        geo_ref[...] = geo
        c8, s8 = cos_sin_turns(geo * (8.0 * df / SPEED_LIGHT))
        stepc_ref[...] = c8
        steps_ref[...] = s8
        at = lax.broadcasted_iota(jnp.int32, (sd, vis_total), 0) + j * sd
        hit = (at == visible_ref[...]).astype(F32).astype(BF16)
        weight = dot_t(jnp.ones((8, vis_total), BF16), hit)[0:1]
        chan = lax.broadcasted_iota(jnp.int32, (kd, sd), 0) + chan_base
        freq = START_FREQ + chan.astype(F32) * df
        amp_ref[...] = (
            jnp.sqrt(bright_ref[...] * jnp.exp(-spec_ref[...] * jnp.log(freq / PIVOT_FREQ)))
            * weight
        )
        ids = lax.broadcasted_iota(jnp.int32, (na, nbl), 0)
        oa_ref[...] = (ids == pairs_ref[0:1, :]).astype(F32).astype(BF16)
        ob_ref[...] = (ids == pairs_ref[1:2, :]).astype(F32)
        owner = group_ref[...] // GD
        mine = lax.broadcasted_iota(jnp.int32, (nf * ns, nbl), 0) == owner
        mine_f = mine.astype(F32)
        before = lax.broadcasted_iota(jnp.int32, (nbl, nbl), 0) < lax.broadcasted_iota(
            jnp.int32, (nbl, nbl), 1
        )
        counts = jnp.dot(
            mine_f.astype(BF16), before.astype(F32).astype(BF16), preferred_element_type=F32
        )
        rank = jnp.sum(counts * mine_f, axis=0, keepdims=True).astype(jnp.int32)
        slot = ((owner % ns) * nf + owner // ns) * SLOTS + rank
        for b in range(ns):
            place = lax.broadcasted_iota(jnp.int32, (per, nbl), 0) + b * per
            hit_ref[b] = (place == slot).astype(F32).astype(BF16)

    chan8 = lax.broadcasted_iota(jnp.int32, (8, sd), 0) + chan_base
    turn_rate = (START_FREQ + chan8.astype(F32) * df) * (1.0 / SPEED_LIGHT)

    def build(i, carry):
        a = step * ABLK + i
        c, s = cos_sin_turns(geo_ref[pl.ds(a, 1), :] * turn_rate)
        cd = stepc_ref[pl.ds(a, 1), :]
        sdl = steps_ref[pl.ds(a, 1), :]
        cs, ss = [c], [s]
        for _ in range(kd // 8 - 1):
            c, s = c * cd - s * sdl, s * cd + c * sdl
            cs.append(c)
            ss.append(s)
        amp = amp_ref[...]
        ca = jnp.concatenate(cs, axis=0) * amp
        sa = jnp.concatenate(ss, axis=0) * amp
        rows = pl.ds(pl.multiple_of(a * (kd + PAD), 8), kd)
        for pq in range(4):
            br = jones_ref[0, i, pq].astype(F32)
            bi = jones_ref[0, i, 4 + pq].astype(F32)
            zbuf[pq, rows, :] = br * ca + bi * sa
            zbuf[4 + pq, rows, :] = bi * ca - br * sa
        return carry

    lax.fori_loop(0, ABLK, build, 0, unroll=4)

    @pl.when(step == steps - 1)
    def _():
        def channel(h, k, carry):
            def z(r, p, q):
                return zbuf[
                    4 * r + 2 * p + q, pl.ds(h * KC + k, na, stride=kd + PAD), :
                ].astype(BF16)

            zr = jnp.concatenate(
                [jnp.concatenate([z(0, p, 0), z(0, p, 1)], axis=1) for p in range(2)], axis=0
            )
            zi = jnp.concatenate(
                [jnp.concatenate([z(1, p, 0), z(1, p, 1)], axis=1) for p in range(2)], axis=0
            )
            left = jnp.concatenate([zr, zi], axis=1)
            turned = jnp.concatenate([zi, -zr], axis=1)
            oa = oa_ref[...]
            ob = ob_ref[...]
            rows = []
            for right in (left, turned):
                gram = dot_t(left, right).astype(BF16)
                for p in range(2):
                    picked = jnp.dot(
                        gram[:, p * na : (p + 1) * na], oa, preferred_element_type=F32
                    )
                    for p2 in range(2):
                        rows.append(
                            jnp.sum(
                                picked[p2 * na : (p2 + 1) * na] * ob, axis=0, keepdims=True
                            )
                        )
            vis = jnp.concatenate(rows, axis=0)
            for t in range(nbl // 128):
                vbuf[t, pl.ds(k, 8, stride=KC), :] = vis[:, t * 128 : (t + 1) * 128]
            return carry

        chunks = kd // KC
        first = [[] for _ in range(chunks)]
        second = [[] for _ in range(chunks)]

        def send_src(h):
            for o in range(1, ns):
                to = lax.rem(j + o, ns)
                copy = pltpu.make_async_remote_copy(
                    src_ref=wbuf.at[h, to],
                    dst_ref=rbuf.at[h, o - 1],
                    send_sem=send1.at[h, o - 1],
                    recv_sem=recv1.at[h, o - 1],
                    device_id=(f, to),
                    device_id_type=MESH,
                )
                copy.start()
                first[h].append(copy)

        def send_freq(h):
            total = wbuf[h, j].astype(F32)
            for o in range(1, ns):
                first[h][o - 1].wait_recv()
                total = total + rbuf[h, o - 1].astype(F32)
            sbuf[h] = total.reshape(nf, SLOTS, 8 * KC)
            for o in range(1, nf):
                to = lax.rem(f + o, nf)
                copy = pltpu.make_async_remote_copy(
                    src_ref=sbuf.at[h, to],
                    dst_ref=dbuf.at[h, f],
                    send_sem=send2.at[h, o - 1],
                    recv_sem=recv2.at[h, o - 1],
                    device_id=(to, j),
                    device_id_type=MESH,
                )
                copy.start()
                second[h].append(copy)
            dbuf[h, f] = sbuf[h, f]

        def transform(h):
            for copy in second[h]:
                copy.wait_recv()
            blocks = [dbuf[h, i] for i in range(nf)]
            vis = jnp.concatenate(
                [
                    jnp.concatenate([b[:, c * KC : (c + 1) * KC] for b in blocks], axis=1)
                    for c in range(8)
                ],
                axis=0,
            )
            return jnp.dot(vis, table_ref[h], precision=HIGHEST, preferred_element_type=F32)

        for h in range(chunks):
            lax.fori_loop(0, KC, functools.partial(channel, h), 0, unroll=8)
            vals = jnp.concatenate([vbuf[t] for t in range(nbl // 128)], axis=1).astype(BF16)
            for b in range(ns):
                wbuf[h, b] = dot_t(hit_ref[b], vals).astype(BF16)
            if h == 0:
                pl.semaphore_wait(barrier, ns + nf - 2)
            send_src(h)
        dev = f * ns + j
        groups = group_ref[...]
        shape = (8, 4 * SLOTS)
        row = lax.broadcasted_iota(jnp.int32, shape, 0)
        col = lax.broadcasted_iota(jnp.int32, shape, 1)
        mean = jnp.zeros(shape, F32)
        start = jnp.zeros((1, 1), F32)
        slot = (col % SLOTS).astype(F32)
        for g in range(GD):
            count = jnp.sum((groups == dev * GD + g).astype(F32), axis=1, keepdims=True)
            inside = (row // 4 == g) & (row % 4 == col // SLOTS)
            inside = inside & (slot >= start) & (slot < start + count)
            mean = mean + jnp.where(inside, 1.0 / (count * scale), 0.0)
            start = start + count
        both = 0.0
        for h in range(chunks):
            send_freq(h)
            if h < chunks - 1:
                both = both + transform(h)
        both = both + transform(chunks - 1)
        nu = table_ref.shape[2] // 2
        half = 4 * SLOTS
        real = both[:half, :nu] + both[half:, nu:]
        imag = both[half:, :nu] - both[:half, nu:]
        power = real * real + imag * imag
        out_ref[...] = jnp.dot(mean, power, precision=HIGHEST, preferred_element_type=F32)
        for h in range(chunks):
            for copy in first[h] + second[h]:
                copy.wait_send()


def fused(nf, ns, chan_count, scale, jones, *small):
    na, kd, sd = jones.shape[1], jones.shape[3], jones.shape[4]
    nbl = small[5].shape[1]
    chunks = kd // KC
    per = nf * SLOTS
    whole = lambda x: pl.BlockSpec(x.shape, lambda i: (0,) * x.ndim)
    return pl.pallas_call(
        functools.partial(kernel, nf, ns, chan_count, scale),
        grid=(na // ABLK,),
        out_shape=jax.ShapeDtypeStruct((8, chan_count), F32),
        in_specs=[pl.BlockSpec((1, ABLK, 8, kd, sd), lambda i: (0, i, 0, 0, 0))]
        + [whole(x) for x in small],
        out_specs=pl.BlockSpec((8, chan_count), lambda i: (0, 0)),
        scratch_shapes=[
            pltpu.VMEM((8, na * (kd + PAD), sd), F32),
            pltpu.VMEM((na, sd), F32),
            pltpu.VMEM((na, sd), F32),
            pltpu.VMEM((na, sd), F32),
            pltpu.VMEM((kd, sd), F32),
            pltpu.VMEM((na, nbl), BF16),
            pltpu.VMEM((na, nbl), F32),
            pltpu.VMEM((ns, per, nbl), BF16),
            pltpu.VMEM((nbl // 128, 8 * KC, 128), F32),
            pltpu.VMEM((chunks, ns, per, 8 * KC), BF16),
            pltpu.VMEM((chunks, ns - 1, per, 8 * KC), BF16),
            pltpu.VMEM((chunks, nf, SLOTS, 8 * KC), F32),
            pltpu.VMEM((chunks, nf, SLOTS, 8 * KC), F32),
            pltpu.SemaphoreType.DMA((chunks, ns - 1)),
            pltpu.SemaphoreType.DMA((chunks, ns - 1)),
            pltpu.SemaphoreType.DMA((chunks, nf - 1)),
            pltpu.SemaphoreType.DMA((chunks, nf - 1)),
        ],
        compiler_params=pltpu.CompilerParams(
            collective_id=0, has_side_effects=True, vmem_limit_bytes=60 * 1024 * 1024
        ),
    )(jones, *small)


def delay_table(chan_count, nf):
    k = np.arange(chan_count)
    angles = 2.0 * np.pi * k / chan_count
    taper = (
        0.35875
        - 0.48829 * np.cos(angles)
        + 0.14128 * np.cos(2.0 * angles)
        - 0.01168 * np.cos(3.0 * angles)
    )
    phases = 2.0 * np.pi * ((k[:, None] * k[None, :]) % chan_count) / chan_count
    both = np.concatenate([np.cos(phases), np.sin(phases)], axis=1) * taper[:, None]
    both = both.reshape(nf, -1, KC, 2 * chan_count).transpose(1, 0, 2, 3)
    return both.reshape(-1, nf * KC, 2 * chan_count).astype(np.float32)


def per_device(nf, ns, jones, directions, brightness, spectral, antennas, visible, pairs, group_of):
    chan_count = jones.shape[3] * nf
    groups = group_of.reshape(1, -1)
    table = jnp.asarray(delay_table(chan_count, nf))
    out = fused(
        nf, ns, chan_count, float(visible.shape[1] * chan_count), jones, directions,
        brightness.reshape(1, -1), spectral.reshape(1, -1), antennas, visible, pairs, groups, table,
    )
    return out.reshape(GD, 1, 4, chan_count)


def solution(mesh):
    nf, ns = mesh.shape["freq"], mesh.shape["src"]
    return jax.shard_map(
        functools.partial(per_device, nf, ns),
        mesh=mesh,
        in_specs=(
            P(None, None, None, "freq", "src"),
            P(None, None, "src"),
            P("src"),
            P("src"),
            P(),
            P(),
            P(),
            P(),
        ),
        out_specs=P(("freq", "src"), None, None, None),
        check_vma=False,
    )
```

```python
import functools
import math

import jax
import jax.numpy as jnp
import numpy as np
from jax import lax
from jax.experimental import pallas as pl
from jax.experimental.pallas import tpu as pltpu
from jax.sharding import PartitionSpec as P

GD = 2
SLOTS = 16
SPEED_LIGHT = 299792458.0
START_FREQ = 100000000.0
BAND_WIDTH = 100000000.0
PIVOT_FREQ = 150000000.0
HIGHEST = lax.Precision.HIGHEST
F32 = jnp.float32
BF16 = jnp.bfloat16
MESH = pl.DeviceIdType.MESH
BLOCKS = 8
PARTS = 2
KC = 16
PAD = 8

SIN_C = [(-1.0) ** i / math.factorial(2 * i + 1) for i in range(6)]
COS_C = [(-1.0) ** i / math.factorial(2 * i) for i in range(7)]


def dot_t(a, b):
    return lax.dot_general(a, b, (((1,), (1,)), ((), ())), preferred_element_type=F32)


def cos_sin_turns(x):
    r = x - jnp.round(x)
    h = r * math.pi
    h2 = h * h
    s = SIN_C[-1]
    for c in SIN_C[-2::-1]:
        s = s * h2 + c
    s = s * h
    c_ = COS_C[-1]
    for c in COS_C[-2::-1]:
        c_ = c_ * h2 + c
    s2 = s + s
    return 1.0 - s2 * s, s2 * c_


def kernel(
    nf, ns, chan_count, scale,
    jones_ref, *refs,
):
    small_hbm, out_ref = refs[:8], refs[8]
    dir_ref, bright_ref, spec_ref, ant_ref, visible_ref, pairs_ref, group_ref, table_ref = refs[
        9:17
    ]
    (
        jbuf, geo_ref, stepc_ref, steps_ref, amp_ref, oa_ref, ob_ref, hit_ref, vbuf,
        wbuf, rbuf, sbuf, dbuf, small_sem, jones_sem, send1, recv1, send2, recv2,
    ) = refs[17:36]
    zbufs = refs[36:]
    na = ant_ref.shape[1]
    kd = jones_ref.shape[3]
    chunks = kd // KC
    sd = jones_ref.shape[4]
    nbl = pairs_ref.shape[1]
    vis_total = visible_ref.shape[1]
    per = nf * SLOTS
    df = BAND_WIDTH / chan_count
    f = lax.axis_index("freq")
    j = lax.axis_index("src")
    chan_base = f * kd
    barrier = pltpu.get_barrier_semaphore()

    for o in range(1, ns):
        pl.semaphore_signal(
            barrier, inc=1, device_id=(f, lax.rem(j + o, ns)), device_id_type=MESH
        )
    for o in range(1, nf):
        pl.semaphore_signal(
            barrier, inc=1, device_id=(lax.rem(f + o, nf), j), device_id_type=MESH
        )
    small_copies = [
        pltpu.make_async_copy(x, y, small_sem.at[i])
        for i, (x, y) in enumerate(zip(small_hbm, refs[9:17]))
    ]
    for copy in small_copies[:-1]:
        copy.start()
    ab = na // BLOCKS

    def beams(h, i):
        return pltpu.make_async_copy(
            jones_ref.at[0, pl.ds(i * ab, ab), :, pl.ds(h * KC, KC), :],
            jbuf.at[h, pl.ds(i * ab, ab)],
            jones_sem.at[h, i],
        )

    for h in range(chunks):
        for i in range(BLOCKS):
            beams(h, i).start()
    small_copies[-1].start()
    for copy in small_copies[:-1]:
        copy.wait()
    ants = jnp.transpose(
        jnp.concatenate([ant_ref[...], jnp.zeros((na - 3, na), F32)], axis=0)
    )
    dirs = [dir_ref[:, i * sd : (i + 1) * sd] for i in range(3)]
    geo = (
        ants[:, 0:1] * dirs[0]
        + ants[:, 1:2] * dirs[1]
        + ants[:, 2:3] * dirs[2]
    )
    geo_ref[...] = geo
    c8, s8 = cos_sin_turns(geo * (8.0 * df / SPEED_LIGHT))
    stepc_ref[...] = c8
    steps_ref[...] = s8
    at = lax.broadcasted_iota(jnp.int32, (sd, vis_total), 0) + j * sd
    hit = (at == visible_ref[...]).astype(F32).astype(BF16)
    weight = dot_t(jnp.ones((8, vis_total), BF16), hit)[0:1]
    chan = lax.broadcasted_iota(jnp.int32, (kd, sd), 0) + chan_base
    freq = START_FREQ + chan.astype(F32) * df
    amp_ref[...] = (
        jnp.sqrt(bright_ref[...] * jnp.exp(-spec_ref[...] * jnp.log(freq / PIVOT_FREQ)))
        * weight
    )
    ids = lax.broadcasted_iota(jnp.int32, (na, nbl), 0)
    oa_ref[...] = (ids == pairs_ref[0:1, :]).astype(F32).astype(BF16)
    ob_ref[...] = (ids == pairs_ref[1:2, :]).astype(F32)
    owner = group_ref[...] // GD
    mine = lax.broadcasted_iota(jnp.int32, (nf * ns, nbl), 0) == owner
    mine_f = mine.astype(F32)
    before = lax.broadcasted_iota(jnp.int32, (nbl, nbl), 0) < lax.broadcasted_iota(
        jnp.int32, (nbl, nbl), 1
    )
    counts = jnp.dot(
        mine_f.astype(BF16), before.astype(F32).astype(BF16), preferred_element_type=F32
    )
    rank = jnp.sum(counts * mine_f, axis=0, keepdims=True).astype(jnp.int32)
    slot = ((owner % ns) * nf + owner // ns) * SLOTS + rank
    for b in range(ns):
        place = lax.broadcasted_iota(jnp.int32, (per, nbl), 0) + b * per
        hit_ref[b] = (place == slot).astype(F32).astype(BF16)

    chan8 = lax.broadcasted_iota(jnp.int32, (8, sd), 0) + chan_base

    def build(h, a):
        rate = (START_FREQ + (chan8 + h * KC).astype(F32) * df) * (1.0 / SPEED_LIGHT)
        c, s = cos_sin_turns(geo_ref[pl.ds(a, 1), :] * rate)
        cd = stepc_ref[pl.ds(a, 1), :]
        sdl = steps_ref[pl.ds(a, 1), :]
        cs, ss = [c], [s]
        for _ in range(KC // 8 - 1):
            c, s = c * cd - s * sdl, s * cd + c * sdl
            cs.append(c)
            ss.append(s)
        amp = amp_ref[h * KC : (h + 1) * KC]
        ca = jnp.concatenate(cs, axis=0) * amp
        sa = jnp.concatenate(ss, axis=0) * amp
        rows = pl.ds(pl.multiple_of(a * (KC + PAD), 8), KC)
        for pq in range(4):
            br = jbuf[h, a, pq].astype(F32)
            bi = jbuf[h, a, 4 + pq].astype(F32)
            zbufs[h][pq, rows, :] = br * ca + bi * sa
            zbufs[h][4 + pq, rows, :] = bi * ca - br * sa

    def build_first(i, carry):
        build(0, i)
        return carry

    for i in range(BLOCKS):
        beams(0, i).wait()
        lax.fori_loop(i * ab, (i + 1) * ab, build_first, 0, unroll=8)

    def channel(h, k):
        def z(r, p, q):
            return zbufs[h][
                4 * r + 2 * p + q, pl.ds(k, na, stride=KC + PAD), :
            ].astype(BF16)

        zr = jnp.concatenate(
            [jnp.concatenate([z(0, p, 0), z(0, p, 1)], axis=1) for p in range(2)], axis=0
        )
        zi = jnp.concatenate(
            [jnp.concatenate([z(1, p, 0), z(1, p, 1)], axis=1) for p in range(2)], axis=0
        )
        left = jnp.concatenate([zr, zi], axis=1)
        both = jnp.concatenate([left, jnp.concatenate([-zi, zr], axis=1)], axis=0)
        gram = dot_t(both, left).astype(BF16)
        gram = jnp.concatenate([gram[:, :na], gram[:, na:]], axis=0)
        picked = jnp.dot(gram, oa_ref[...], preferred_element_type=F32)
        ob = ob_ref[...]
        rows = []
        for r in range(2):
            for p in range(2):
                for p2 in range(2):
                    at = ((p * 2 + r) * 2 + p2) * na
                    rows.append(
                        jnp.sum(picked[at : at + na] * ob, axis=0, keepdims=True)
                    )
        vis = jnp.concatenate(rows, axis=0)
        for t in range(nbl // 128):
            vbuf[t, pl.ds(k, 8, stride=KC), :] = vis[:, t * 128 : (t + 1) * 128]

    batch = KC // PARTS

    def channels(h, t, carry):
        if h + 1 < chunks:
            for i in range(BLOCKS // PARTS):
                beams(h + 1, t * (BLOCKS // PARTS) + i).wait()
        for u in range(batch):
            channel(h, t * batch + u)
            if h + 1 < chunks:
                for v in range(na // KC):
                    build(h + 1, (t * batch + u) * (na // KC) + v)
        return carry

    first = [[] for _ in range(chunks)]
    second = [[] for _ in range(chunks)]

    def send_src(h):
        for o in range(1, ns):
            to = lax.rem(j + o, ns)
            copy = pltpu.make_async_remote_copy(
                src_ref=wbuf.at[h, to],
                dst_ref=rbuf.at[h, o - 1],
                send_sem=send1.at[h, o - 1],
                recv_sem=recv1.at[h, o - 1],
                device_id=(f, to),
                device_id_type=MESH,
            )
            copy.start()
            first[h].append(copy)

    def send_freq(h):
        total = wbuf[h, j].astype(F32)
        for o in range(1, ns):
            first[h][o - 1].wait_recv()
            total = total + rbuf[h, o - 1].astype(F32)
        sbuf[h] = total.reshape(nf, SLOTS, 8 * KC)
        for o in range(1, nf):
            to = lax.rem(f + o, nf)
            copy = pltpu.make_async_remote_copy(
                src_ref=sbuf.at[h, to],
                dst_ref=dbuf.at[h, f],
                send_sem=send2.at[h, o - 1],
                recv_sem=recv2.at[h, o - 1],
                device_id=(to, j),
                device_id_type=MESH,
            )
            copy.start()
            second[h].append(copy)
        dbuf[h, f] = sbuf[h, f]

    def transform(h):
        for copy in second[h]:
            copy.wait_recv()
        blocks = [dbuf[h, i] for i in range(nf)]
        vis = jnp.concatenate(
            [
                jnp.concatenate([b[:, c * KC : (c + 1) * KC] for b in blocks], axis=1)
                for c in range(8)
            ],
            axis=0,
        )
        return jnp.dot(vis, table_ref[h], precision=HIGHEST, preferred_element_type=F32)

    for h in range(chunks):
        lax.fori_loop(0, PARTS, functools.partial(channels, h), 0)
        vals = jnp.concatenate([vbuf[t] for t in range(nbl // 128)], axis=1).astype(BF16)
        for b in range(ns):
            wbuf[h, b] = dot_t(hit_ref[b], vals).astype(BF16)
        if h == 0:
            pl.semaphore_wait(barrier, ns + nf - 2)
        send_src(h)
    dev = f * ns + j
    groups = group_ref[...]
    shape = (8, 4 * SLOTS)
    row = lax.broadcasted_iota(jnp.int32, shape, 0)
    col = lax.broadcasted_iota(jnp.int32, shape, 1)
    mean = jnp.zeros(shape, F32)
    start = jnp.zeros((1, 1), F32)
    slot = (col % SLOTS).astype(F32)
    for g in range(GD):
        count = jnp.sum((groups == dev * GD + g).astype(F32), axis=1, keepdims=True)
        inside = (row // 4 == g) & (row % 4 == col // SLOTS)
        inside = inside & (slot >= start) & (slot < start + count)
        mean = mean + jnp.where(inside, 1.0 / (count * scale), 0.0)
        start = start + count
    small_copies[-1].wait()
    both = 0.0
    for h in range(chunks):
        send_freq(h)
        if h < chunks - 1:
            both = both + transform(h)
    both = both + transform(chunks - 1)
    nu = table_ref.shape[2] // 2
    half = 4 * SLOTS
    real = both[:half, :nu] + both[half:, nu:]
    imag = both[half:, :nu] - both[:half, nu:]
    power = real * real + imag * imag
    out_ref[...] = jnp.dot(mean, power, precision=HIGHEST, preferred_element_type=F32)
    for h in range(chunks):
        for copy in first[h] + second[h]:
            copy.wait_send()


def fused(nf, ns, chan_count, scale, jones, *small):
    na, kd, sd = jones.shape[1], jones.shape[3], jones.shape[4]
    nbl = small[5].shape[1]
    chunks = kd // KC
    per = nf * SLOTS
    return pl.pallas_call(
        functools.partial(kernel, nf, ns, chan_count, scale),
        grid=(1,),
        out_shape=jax.ShapeDtypeStruct((8, chan_count), F32),
        in_specs=[pl.BlockSpec(memory_space=pl.ANY)] * (1 + len(small)),
        out_specs=pl.BlockSpec((8, chan_count), lambda i: (0, 0)),
        scratch_shapes=[pltpu.VMEM(x.shape, x.dtype) for x in small]
        + [
            pltpu.VMEM((chunks, na, 8, KC, sd), BF16),
            pltpu.VMEM((na, sd), F32),
            pltpu.VMEM((na, sd), F32),
            pltpu.VMEM((na, sd), F32),
            pltpu.VMEM((kd, sd), F32),
            pltpu.VMEM((na, nbl), BF16),
            pltpu.VMEM((na, nbl), F32),
            pltpu.VMEM((ns, per, nbl), BF16),
            pltpu.VMEM((nbl // 128, 8 * KC, 128), F32),
            pltpu.VMEM((chunks, ns, per, 8 * KC), BF16),
            pltpu.VMEM((chunks, ns - 1, per, 8 * KC), BF16),
            pltpu.VMEM((chunks, nf, SLOTS, 8 * KC), F32),
            pltpu.VMEM((chunks, nf, SLOTS, 8 * KC), F32),
            pltpu.SemaphoreType.DMA((len(small),)),
            pltpu.SemaphoreType.DMA((chunks, BLOCKS)),
            pltpu.SemaphoreType.DMA((chunks, ns - 1)),
            pltpu.SemaphoreType.DMA((chunks, ns - 1)),
            pltpu.SemaphoreType.DMA((chunks, nf - 1)),
            pltpu.SemaphoreType.DMA((chunks, nf - 1)),
        ]
        + [pltpu.VMEM((8, na * (KC + PAD), sd), F32)] * chunks,
        compiler_params=pltpu.CompilerParams(
            collective_id=0, has_side_effects=True, vmem_limit_bytes=60 * 1024 * 1024
        ),
    )(jones, *small)


def delay_table(chan_count, nf):
    k = np.arange(chan_count)
    angles = 2.0 * np.pi * k / chan_count
    taper = (
        0.35875
        - 0.48829 * np.cos(angles)
        + 0.14128 * np.cos(2.0 * angles)
        - 0.01168 * np.cos(3.0 * angles)
    )
    phases = 2.0 * np.pi * ((k[:, None] * k[None, :]) % chan_count) / chan_count
    both = np.concatenate([np.cos(phases), np.sin(phases)], axis=1) * taper[:, None]
    both = both.reshape(nf, -1, KC, 2 * chan_count).transpose(1, 0, 2, 3)
    return both.reshape(-1, nf * KC, 2 * chan_count).astype(np.float32)


def per_device(nf, ns, jones, directions, brightness, spectral, antennas, visible, pairs, group_of):
    chan_count = jones.shape[3] * nf
    groups = group_of.reshape(1, -1)
    table = jnp.asarray(delay_table(chan_count, nf))
    out = fused(
        nf, ns, chan_count, float(visible.shape[1] * chan_count), jones, directions.reshape(1, -1),
        brightness.reshape(1, -1), spectral.reshape(1, -1), antennas, visible, pairs, groups, table,
    )
    return out.reshape(GD, 1, 4, chan_count)


def solution(mesh):
    nf, ns = mesh.shape["freq"], mesh.shape["src"]
    return jax.shard_map(
        functools.partial(per_device, nf, ns),
        mesh=mesh,
        in_specs=(
            P(None, None, None, "freq", "src"),
            P(None, None, "src"),
            P("src"),
            P("src"),
            P(),
            P(),
            P(),
            P(),
        ),
        out_specs=P(("freq", "src"), None, None, None),
        check_vma=False,
    )
```
